256 devices in a mesh: row: 16 (over y, x), col: 16 (over z, core).
Axes of the slice: x: 4, y: 4, z: 8, core: 2. Of those that a mesh axis runs over, the one named last changes fastest.
Arguments:
- fisher: float32 [16, 512, 16, 512], P('row', None, 'col'), may hold values from -2 to 4, as said below
Outputs:
- reduced: float32 [16, 512, 16, 512], P('row', None, 'col')
The draws below stay inside these ranges and needn't reach their ends.
Inputs may be any that keep to these rules, and one draw needn't show every extreme that they name: `fisher`: M is symmetric and positive definite, so that every pivot met is positive definite; its diagonal entries lie in 2.5 to 4.
All inputs are finite; a program needn't handle non-finite values.
Results may differ from the reference program's by a relative error of at most 0.0001.
Values sent between devices are 32-bit elements; how exact they have to be, the bound alone decides.
No kernel may reach another device: no remote copies, remote signals or barrier semaphores. Data moves between devices by JAX's collectives and lax.ppermute only.
A program may use at most 64 MiB of HBM per device.

```python
import jax
import jax.numpy as jnp
from jax import lax

TILE = 512
STEPS = 3
ORDER = 8192
LR = 1
LC = 1
N_ROW = 16
N_COL = 16


def draw_fisher(key, part):
    key = jax.random.fold_in(key, 11)
    first, second = jax.random.split(key)
    index = jnp.arange(ORDER)
    same_tile = index[:, None] // TILE == index[None, :] // TILE
    spread = jnp.sqrt(jnp.where(same_tile, 0.25 / TILE + 0.75 / ORDER, 0.75 / ORDER))
    noise = jnp.clip(jax.random.normal(first, (ORDER, ORDER), jnp.float32), -6.0, 6.0)
    diagonal = jax.random.uniform(second, (ORDER,), jnp.float32, 2.5, 4.0)
    sym = (noise + noise.T) * 0.70710677 * spread
    where_diag = index[:, None] == index[None, :]
    full = jnp.where(where_diag, diagonal[None, :], sym)
    shaped = full.reshape(LR, N_ROW, TILE, LC, N_COL, TILE)
    return shaped.transpose(1, 0, 2, 4, 3, 5).reshape(N_ROW, LR * TILE, N_COL, LC * TILE)


def setup_inputs(seed: int = 0) -> dict:
    arg_keys = jax.random.split(jax.random.key(seed), 2)
    return {
        "fisher": draw_fisher(jax.random.fold_in(arg_keys[1], 71), 0),
    }


def from_layout(fisher):
    shaped = fisher.reshape(N_ROW, LR, TILE, N_COL, LC, TILE)
    return shaped.transpose(1, 0, 2, 4, 3, 5).reshape(ORDER, ORDER)

def to_layout(matrix):
    shaped = matrix.reshape(LR, N_ROW, TILE, LC, N_COL, TILE)
    return shaped.transpose(1, 0, 2, 4, 3, 5).reshape(N_ROW, LR * TILE, N_COL, LC * TILE)

def invert_pivot(pivot):
    factor = jnp.linalg.cholesky(pivot)
    ident = jnp.eye(pivot.shape[0], dtype=pivot.dtype)
    lower_inv = jax.scipy.linalg.solve_triangular(factor, ident, lower=True)
    return jnp.dot(lower_inv.T, lower_inv, precision=lax.Precision.HIGHEST)

def reference(fisher):
    matrix = from_layout(fisher)
    for step in range(STEPS):
        low = step * TILE
        high = low + TILE
        pivot = matrix[low:high, low:high]
        inverse = invert_pivot(pivot)
        row_old = matrix[low:high, :]
        col_old = matrix[:, low:high]
        new_row = jnp.dot(inverse, row_old, precision=lax.Precision.HIGHEST)
        scaled = -jnp.dot(col_old, inverse, precision=lax.Precision.HIGHEST)
        matrix = matrix - jnp.dot(col_old, new_row, precision=lax.Precision.HIGHEST)
        matrix = matrix.at[low:high, :].set(new_row)
        matrix = matrix.at[:, low:high].set(scaled)
        matrix = matrix.at[low:high, low:high].set(inverse)
    return to_layout(matrix)
```

```python
import jax
import jax.numpy as jnp
from jax import lax
from jax.experimental import pallas as pl
from jax.experimental.pallas import tpu as pltpu
from jax.sharding import PartitionSpec as P

TILE = 512
F32 = jnp.float32
BF16 = jnp.bfloat16
NN = (((1,), (0,)), ((), ()))
NT = (((1,), (1,)), ((), ()))


def halves(value):
    high = value.astype(BF16)
    return high, (value - high.astype(F32)).astype(BF16)


def dot1(left, right):
    return lax.dot_general(left.astype(BF16), right.astype(BF16), NN, preferred_element_type=F32)


def dot3(left, right, dims=NN):
    lh, ll = left if isinstance(left, tuple) else halves(left)
    rh, rl = right if isinstance(right, tuple) else halves(right)
    low = lax.dot_general(lh, rl, dims, preferred_element_type=F32)
    low += lax.dot_general(ll, rh, dims, preferred_element_type=F32)
    return low + lax.dot_general(lh, rh, dims, preferred_element_type=F32)


def eye_mask():
    rows = lax.broadcasted_iota(jnp.int32, (TILE, TILE), 0)
    cols = lax.broadcasted_iota(jnp.int32, (TILE, TILE), 1)
    return rows == cols


def sweep_inverse(mat, inv_ref):
    inv_ref[...] = mat
    rows = lax.broadcasted_iota(jnp.int32, (TILE, TILE), 0)
    cols = lax.broadcasted_iota(jnp.int32, (TILE, TILE), 1)

    def body(k, carry):
        cur = inv_ref[...]
        col = jnp.sum(jnp.where(cols == k, cur, 0.0), axis=1, keepdims=True)
        row = jnp.sum(jnp.where(rows == k, cur, 0.0), axis=0, keepdims=True)
        pivot = jnp.sum(jnp.where((cols == k) & (rows == k), cur, 0.0))
        rate = 1.0 / pivot
        new = cur - (col * rate) * row
        new = jnp.where(rows == k, row * rate, new)
        new = jnp.where(cols == k, col * rate, new)
        inv_ref[...] = jnp.where((rows == k) & (cols == k), -rate, new)
        return carry

    lax.fori_loop(0, TILE, body, 0)
    inv_ref[...] = -inv_ref[...]


TOL = 1e-5


def spd_inverse(mat_ref, inv_ref):
    mat = mat_ref[...]
    diag = eye_mask()
    ident = jnp.where(diag, 1.0, 0.0).astype(F32)
    kept = jnp.where(diag, mat, 0.0)
    rate_c = 1.0 / jnp.sum(kept, axis=1, keepdims=True)
    rate_r = 1.0 / jnp.sum(kept, axis=0, keepdims=True)
    mat2 = halves(mat)
    inv = jnp.where(diag, rate_r, -(mat * rate_c) * rate_r)
    rest = ident - lax.dot_general(mat2[0], inv.astype(BF16), NN, preferred_element_type=F32)
    inv = inv + dot1(inv, rest)

    def refine(inv):
        rest = ident - dot3(mat2, inv)
        return inv + dot1(inv, rest), jnp.sum(rest * rest)

    inv, _ = refine(inv)
    inv, size = refine(inv)
    inv_ref[...] = inv

    @pl.when(jnp.logical_not(size < TOL))
    def _():
        def more(state):
            now, before, _ = state
            return jnp.logical_not(now < TOL) & (now < 0.5 * before)

        def step(state):
            now, _, count = state
            rest = ident - dot3(halves(mat_ref[...]), inv_ref[...])
            inv_ref[...] += dot1(inv_ref[...], rest)
            return jnp.sum(rest * rest), now, count + 1

        last, _, _ = lax.while_loop(more, step, (size, 4.0 * size, 0))

        @pl.when(jnp.logical_not(last < TOL))
        def _():
            sweep_inverse(mat_ref[...], inv_ref)


def first_kernel(a0, x0):
    spd_inverse(a0.at[0], x0)


def chain_kernel(a0, a1, x0, g10, g20, g21, x1, x2, s11, s22):
    a10h = halves(a0[1])
    a20h = halves(a0[2])
    x0h = halves(x0[...])
    g = dot3(a10h, x0h)
    g10[...] = g
    gh = halves(g)
    s11[...] = a1[0] - dot3(gh, a10h, NT)
    spd_inverse(s11, x1)
    g = dot3(a20h, x0h)
    g20[...] = g
    gh = halves(g)
    s21h = halves(a1[1] - dot3(gh, a10h, NT))
    s22[...] = a1[2] - dot3(gh, a20h, NT)
    g = dot3(s21h, halves(x1[...]))
    g21[...] = g
    s22[...] -= dot3(halves(g), s21h, NT)
    spd_inverse(s22, x2)


def final_kernel(place, block, b, c, g10, g20, g21, x0, x1, x2, out):
    row = place[0]
    col = place[1]
    ident = jnp.where(eye_mask(), 1.0, 0.0).astype(F32)

    def rowside(k):
        return jnp.where(row < 3, jnp.where(row == k, -1.0, 0.0) * ident, c[k])

    def colside(k):
        return jnp.where(col < 3, jnp.where(col == k, 1.0, 0.0) * ident, b[k])

    g10h = halves(g10[...])
    f0 = halves(rowside(0))
    v0 = halves(colside(0))
    total = jnp.where((row < 3) | (col < 3), 0.0, block[...])
    total -= dot3(f0, dot3(x0[...], v0))
    f1 = halves(rowside(1) - dot3(f0, g10h, NT))
    v1 = halves(colside(1) - dot3(g10h, v0))
    total -= dot3(f1, dot3(x1[...], v1))
    g20h = halves(g20[...])
    g21h = halves(g21[...])
    f2 = halves(rowside(2) - dot3(f0, g20h, NT) - dot3(f1, g21h, NT))
    v2 = halves(colside(2) - dot3(g20h, v0) - dot3(g21h, v1))
    out[...] = total - dot3(f2, dot3(x2[...], v2))


TILE_F32 = jax.ShapeDtypeStruct((TILE, TILE), F32)
VM = pl.BlockSpec(memory_space=pltpu.VMEM)
SM = pl.BlockSpec(memory_space=pltpu.SMEM)
ROOM = pltpu.CompilerParams(vmem_limit_bytes=40 * 1024 * 1024)


def first(a0):
    return pl.pallas_call(first_kernel, out_shape=TILE_F32, in_specs=[VM], out_specs=VM, compiler_params=ROOM, name="first")(a0)


def chain(*args):
    return pl.pallas_call(
        chain_kernel,
        out_shape=[TILE_F32] * 5,
        in_specs=[VM] * 3,
        out_specs=[VM] * 5,
        scratch_shapes=[pltpu.VMEM((TILE, TILE), F32)] * 2,
        compiler_params=ROOM,
        name="chain",
    )(*args)


def final(*args):
    return pl.pallas_call(
        final_kernel, out_shape=TILE_F32, in_specs=[SM] + [VM] * 9, out_specs=VM, compiler_params=ROOM, name="final"
    )(*args)


N = 16


def line(pairs):
    return [(2 * a % N + h, 2 * b % N + h) for a, b in pairs for h in (0, 1)]


def x_shift(d):
    return [(y * 4 + x, y * 4 + (x + d) % 4) for y in range(4) for x in range(4)]


def y_shift(d):
    return [(y * 4 + x, (y + d) % 4 * 4 + x) for y in range(4) for x in range(4)]


def gather_ring(part, axis, shift, place):
    out = jnp.zeros(part.shape[:axis] + (4,) + part.shape[axis:], part.dtype)
    out = lax.dynamic_update_index_in_dim(out, part, place, axis)
    for d in (1, 3, 2):
        got = lax.ppermute(part, "row", shift(d))
        out = lax.dynamic_update_index_in_dim(out, got, (place - d) % 4, axis)
    return out


def gather_plane(part, x, y):
    line_x = gather_ring(part, 1, x_shift, x)
    both = gather_ring(line_x, 1, y_shift, y)
    return both.reshape(part.shape[0], TILE, TILE)


def spread_line(value, z, root):
    half = value.shape[0] // 2
    at = (z - root) % 8
    got = lax.ppermute(value, "col", line([(root, root + 4)]))
    value = jnp.where(at == 4, got, value)
    up, down = value[:half], value[half:]
    gu = lax.ppermute(up, "col", line([(root, root + 2), (root + 4, root + 6)]))
    gd = lax.ppermute(down, "col", line([(root, root + 6), (root + 4, root + 2)]))
    fresh = (at == 2) | (at == 6)
    up, down = jnp.where(fresh, gu, up), jnp.where(fresh, gd, down)
    gu = lax.ppermute(up, "col", line([(root + i, root + i + 1) for i in (0, 2, 4, 6)]))
    gd = lax.ppermute(down, "col", line([(root + i, root + i - 1) for i in (0, 2, 4, 6)]))
    fresh = at % 2 == 1
    return jnp.concatenate([jnp.where(fresh, gu, up), jnp.where(fresh, gd, down)])


SWAP = [(c, c ^ 1) for c in range(N)]


def on_device(fisher):
    block = fisher[0, :, 0, :]
    row = lax.axis_index("row")
    col = lax.axis_index("col")
    x, y, z, core = row % 4, row // 4, col // 2, col % 2

    slabs = lax.all_to_all(block, "row", 0, 0, tiled=True).reshape(N, 32, TILE)[:3]
    corner = lax.ppermute(slabs[2], "col", [(2, 1)])
    pack = jnp.where(col == 1, jnp.stack([slabs[1], slabs[2], corner]), slabs)
    near = lax.ppermute(pack, "col", line([(0, 2)]))
    back = lax.ppermute(pack, "col", line([(0, 6)]))
    far = lax.ppermute(pack, "col", line([(0, 4)]))
    pack = jnp.where(z == 0, pack, near + back + far)
    odd = lax.ppermute(pack, "col", line([(i, i + 1) for i in (0, 2, 4, 6)]))
    pack = jnp.where(z % 2 == 1, odd, pack)
    mine = gather_plane(pack, x, y)
    other = lax.ppermute(mine, "col", SWAP)
    a0 = jnp.where(core == 0, mine, other)
    a1 = jnp.where(core == 0, other, mine)

    b = gather_plane(slabs, x, y)

    top, bottom = block[:256], block[256:]
    kept = jnp.where(core == 0, top, bottom)
    got = lax.ppermute(jnp.where(core == 0, bottom, top), "col", SWAP)
    even = jnp.where(core == 0, kept, got)
    odd = jnp.where(core == 0, got, kept)
    pair = spread_line(jnp.concatenate([even, odd]), z, 0)
    last = spread_line(even, z, 1)
    half = jnp.concatenate([pair, last]).reshape(3, 256, TILE)
    other = lax.ppermute(half, "col", SWAP)
    c = jnp.where(core == 0, jnp.concatenate([half, other], 1), jnp.concatenate([other, half], 1))

    x0 = first(a0)
    g10, g20, g21, x1, x2 = chain(a0, a1, x0)
    out = final(jnp.stack([row, col]).astype(jnp.int32), block, b, c, g10, g20, g21, x0, x1, x2)
    return out[None, :, None, :]


def solution(mesh):
    spec = P("row", None, "col", None)
    return jax.shard_map(on_device, mesh=mesh, in_specs=(spec,), out_specs=spec, check_vma=False)
```

```python
import jax
import jax.numpy as jnp
from jax import lax
from jax.experimental import pallas as pl
from jax.experimental.pallas import tpu as pltpu
from jax.sharding import PartitionSpec as P

TILE = 512
N = 16
SLAB = TILE // N
F32 = jnp.float32
BF16 = jnp.bfloat16
NN = (((1,), (0,)), ((), ()))
NT = (((1,), (1,)), ((), ()))
TN = (((0,), (0,)), ((), ()))


def halves(value):
    high = value.astype(BF16)
    return high, (value - high.astype(F32)).astype(BF16)


def dot1(left, right):
    return lax.dot_general(left.astype(BF16), right.astype(BF16), NN, preferred_element_type=F32)


def dot3(left, right, dims=NN):
    lh, ll = left if isinstance(left, tuple) else halves(left)
    rh, rl = right if isinstance(right, tuple) else halves(right)
    low = lax.dot_general(lh, rl, dims, preferred_element_type=F32)
    low += lax.dot_general(ll, rh, dims, preferred_element_type=F32)
    return low + lax.dot_general(lh, rh, dims, preferred_element_type=F32)


def eye_mask():
    rows = lax.broadcasted_iota(jnp.int32, (TILE, TILE), 0)
    cols = lax.broadcasted_iota(jnp.int32, (TILE, TILE), 1)
    return rows == cols


def sweep_inverse(mat, inv_ref):
    inv_ref[...] = mat
    rows = lax.broadcasted_iota(jnp.int32, (TILE, TILE), 0)
    cols = lax.broadcasted_iota(jnp.int32, (TILE, TILE), 1)

    def body(k, carry):
        cur = inv_ref[...]
        col = jnp.sum(jnp.where(cols == k, cur, 0.0), axis=1, keepdims=True)
        row = jnp.sum(jnp.where(rows == k, cur, 0.0), axis=0, keepdims=True)
        pivot = jnp.sum(jnp.where((cols == k) & (rows == k), cur, 0.0))
        rate = 1.0 / pivot
        new = cur - (col * rate) * row
        new = jnp.where(rows == k, row * rate, new)
        new = jnp.where(cols == k, col * rate, new)
        inv_ref[...] = jnp.where((rows == k) & (cols == k), -rate, new)
        return carry

    lax.fori_loop(0, TILE, body, 0)
    inv_ref[...] = -inv_ref[...]


def exact(left, right, dims=NN):
    return lax.dot_general(left, right, dims, precision=lax.Precision.HIGHEST, preferred_element_type=F32)


def same(value):
    return value


TOL = 1e-5


def quick_inverse(mat_ref, inv_ref, good):
    mat = mat_ref[...]
    diag = eye_mask()
    ident = jnp.where(diag, 1.0, 0.0).astype(F32)
    kept = jnp.where(diag, mat, 0.0)
    rate_c = 1.0 / jnp.sum(kept, axis=1, keepdims=True)
    rate_r = 1.0 / jnp.sum(kept, axis=0, keepdims=True)
    mat2 = halves(mat)
    inv = jnp.where(diag, rate_r, -(mat * rate_c) * rate_r)
    rest = ident - lax.dot_general(mat2[0], inv.astype(BF16), NN, preferred_element_type=F32)
    inv = inv + dot1(inv, rest)
    for _ in range(2):
        rest = ident - dot3(mat2, inv)
        inv = inv + dot1(inv, rest)
    inv_ref[...] = inv

    @pl.when(jnp.logical_not(jnp.sum(rest * rest) < TOL))
    def _():
        good[0] = 0


def chain_kernel(place, mine, other, *rest):
    outs, (good, mat, out_sems), kept = rest[:6], rest[6:9], rest[9:]
    x0, x1, x2, g10, g20, g21 = kept

    def tile(group, k):
        left, right = (mine, other) if group == 0 else (other, mine)
        return jnp.where(place[2] == 0, left[:, k], right[:, k]).reshape(TILE, TILE)

    def second(mm, split):
        a10 = split(tile(0, 1))
        g = mm(a10, split(x0[...]))
        g10[...] = g
        mat[...] = tile(1, 0) - mm(split(g), a10, NT)

    def third(mm, split):
        a10 = split(tile(0, 1))
        a20 = split(tile(0, 2))
        g = mm(a20, split(x0[...]))
        g20[...] = g
        g = split(g)
        s21 = split(tile(1, 1) - mm(g, a10, NT))
        mat[...] = tile(1, 2) - mm(g, a20, NT)
        g = mm(s21, split(x1[...]))
        g21[...] = g
        mat[...] -= mm(split(g), s21, NT)

    good[0] = 1
    mat[...] = tile(0, 0)
    quick_inverse(mat, x0, good)
    second(dot3, halves)
    quick_inverse(mat, x1, good)
    third(dot3, halves)
    quick_inverse(mat, x2, good)

    @pl.when(good[0] == 0)
    def _():
        sweep_inverse(tile(0, 0), x0)
        second(exact, same)
        sweep_inverse(mat[...], x1)
        third(exact, same)
        sweep_inverse(mat[...], x2)

    send = [pltpu.make_async_copy(kept[i], outs[i], out_sems.at[i]) for i in range(6)]
    for copy in send:
        copy.start()
    for copy in send:
        copy.wait()


def fetched(sources, scratch, sems):
    copies = [pltpu.make_async_copy(sources[i], scratch.at[i], sems.at[i]) for i in range(len(sources))]
    for copy in copies:
        copy.start()

    def get(i):
        copies[i].wait()
        return scratch.at[i]

    return get


def row_kernel(place, good, own, far, last, last_far, x0, x1, x2, g10, g20, g21, w0, w1, w2, hold, kept, sems, out_sems):
    row = place[0]
    first_core = place[2] == 0
    get = fetched([own, far, last, last_far, x0, g10, x1, g20, g21, x2], hold, sems)
    own, far, last, last_far, x0, g10, x1, g20, g21, x2 = [get(i) for i in range(10)]

    def finish(mm, split):
        ident = jnp.where(eye_mask(), 1.0, 0.0).astype(F32)

        def rowside(k):
            left, right = ((own, far), (far, own), (last, last_far))[k]
            value = jnp.where(first_core, left[...], right[...])
            return jnp.where(row < 3, jnp.where(row == k, -1.0, 0.0) * ident, value)

        g10h = split(g10[...])
        g20h = split(g20[...])
        g21h = split(g21[...])
        u0 = split(rowside(0))
        kept[0] = mm(u0, split(x0[...]))
        u1 = split(rowside(1) - mm(u0, g10h, NT))
        kept[1] = mm(u1, split(x1[...]))
        u2 = rowside(2) - mm(u0, g20h, NT) - mm(u1, g21h, NT)
        value = mm(split(u2), split(x2[...]))
        kept[2] = value
        part = split(value)
        kept[0] -= mm(part, g20h)
        value = kept[1] - mm(part, g21h)
        kept[1] = value
        kept[0] -= mm(split(value), g10h)

    @pl.when(good[0] == 1)
    def _():
        finish(dot3, halves)

    @pl.when(good[0] == 0)
    def _():
        finish(exact, same)

    send = [pltpu.make_async_copy(kept.at[i], out, out_sems.at[i]) for i, out in enumerate((w0, w1, w2))]
    for copy in send:
        copy.start()
    for copy in send:
        copy.wait()


def final_kernel(place, good, block, b, w0, w1, w2, out, hold, tiles, sems, tile_sems):
    row = place[0]
    col = place[1]
    fetch = [pltpu.make_async_copy(b.at[:, k], tiles.at[k], tile_sems.at[k]) for k in range(3)]
    for copy in fetch:
        copy.start()
    get = fetched([block, w0, w1, w2], hold, sems)
    block, w0, w1, w2 = [get(i) for i in range(4)]
    for copy in fetch:
        copy.wait()

    def finish(mm, split):
        ident = jnp.where(eye_mask(), 1.0, 0.0).astype(F32)

        def colside(k):
            value = tiles[k].reshape(TILE, TILE)
            return jnp.where(col < 3, jnp.where(col == k, 1.0, 0.0) * ident, value)

        total = jnp.where((row < 3) | (col < 3), 0.0, block[...])
        for k, weight in enumerate((w0, w1, w2)):
            total -= mm(split(weight[...]), split(colside(k)))
        out[...] = total

    @pl.when(good[0] == 1)
    def _():
        finish(dot3, halves)

    @pl.when(good[0] == 0)
    def _():
        finish(exact, same)


TILE_F32 = jax.ShapeDtypeStruct((TILE, TILE), F32)
VM = pl.BlockSpec(memory_space=pltpu.VMEM)
SM = pl.BlockSpec(memory_space=pltpu.SMEM)
ANY = pl.BlockSpec(memory_space=pl.ANY)
ROOM = pltpu.CompilerParams(vmem_limit_bytes=36 * 1024 * 1024)


def cost(products):
    return pl.CostEstimate(flops=products * 10**9, bytes_accessed=12 * 2**20, transcendentals=0)


def chain(*args):
    return pl.pallas_call(
        chain_kernel,
        out_shape=[TILE_F32] * 6 + [jax.ShapeDtypeStruct((1,), jnp.int32)],
        in_specs=[SM] + [VM] * 2,
        out_specs=[ANY] * 6 + [SM],
        scratch_shapes=[
            pltpu.VMEM((TILE, TILE), F32),
            pltpu.SemaphoreType.DMA((6,)),
        ]
        + [pltpu.VMEM((TILE, TILE), F32)] * 6,
        compiler_params=ROOM,
        cost_estimate=cost(20),
        name="chain",
    )(*args)


def rows(*args):
    return pl.pallas_call(
        row_kernel,
        out_shape=[TILE_F32] * 3,
        in_specs=[SM] * 2 + [ANY] * 10,
        out_specs=[ANY] * 3,
        scratch_shapes=[
            pltpu.VMEM((10, TILE, TILE), F32),
            pltpu.VMEM((3, TILE, TILE), F32),
            pltpu.SemaphoreType.DMA((10,)),
            pltpu.SemaphoreType.DMA((3,)),
        ],
        compiler_params=ROOM,
        cost_estimate=cost(13),
        name="rows",
    )(*args)


def final(*args):
    return pl.pallas_call(
        final_kernel,
        out_shape=TILE_F32,
        in_specs=[SM] * 2 + [ANY] * 5,
        out_specs=VM,
        scratch_shapes=[
            pltpu.VMEM((4, TILE, TILE), F32),
            pltpu.VMEM((3, N, SLAB, TILE), F32),
            pltpu.SemaphoreType.DMA((4,)),
            pltpu.SemaphoreType.DMA((3,)),
        ],
        compiler_params=ROOM,
        cost_estimate=cost(4),
        name="final",
    )(*args)


def line(pairs, cores):
    return [(2 * a % N + h, 2 * b % N + h) for a, b in pairs for h in cores]


def after(value, *earlier):
    return lax.optimization_barrier((value, earlier))[0]


def plane_gather(part):
    copies = jnp.broadcast_to(part[None], (N,) + part.shape)
    return lax.all_to_all(copies, "row", 0, 0, tiled=True)


SWAP = [(c, c ^ 1) for c in range(N)]


def line_start(value, z, root, cores=(0, 1)):
    fwd = lax.ppermute(value, "col", line([(root, root + 3)], cores))
    back = lax.ppermute(value, "col", line([(root, root + 5)], cores))
    return jnp.where(z == root, value, fwd + back)


def line_end(value, z, root, cores=(0, 1)):
    fwd = lax.ppermute(value, "col", line([(root + i, root + i + 1) for i in (0, 3, 5)], cores))
    back = lax.ppermute(value, "col", line([(root + i, root + i - 1) for i in (0, 3)], cores))
    have = (z == root) | (z == (root + 3) % 8) | (z == (root + 5) % 8)
    return jnp.where(have, value, fwd + back)


def on_device(fisher):
    block = fisher[0, :, 0, :]
    row = lax.axis_index("row")
    col = lax.axis_index("col")
    z, core = col // 2, col % 2
    place = jnp.stack([row, col, core]).astype(jnp.int32)

    with jax.named_scope("c_start"):
        own = line_start(block, z, 0)
        last = line_start(block, z, 1, (0,))
    with jax.named_scope("slabs"):
        slabs = lax.all_to_all(block, "row", 0, 0, tiled=True).reshape(N, SLAB, TILE)[:3]
    with jax.named_scope("a_line"):
        corner = lax.ppermute(slabs[2], "col", [(2, 1)])
        pack = jnp.where(col == 1, jnp.stack([slabs[1], slabs[2], corner]), slabs)
        seed = after(line_start(pack, z, 0), own, last)
        pack = line_end(seed, z, 0)
    with jax.named_scope("c_end"):
        own = line_end(after(own, pack), z, 0)
        last = line_end(after(last, pack), z, 1, (0,))
    with jax.named_scope("a_plane"):
        mine = plane_gather(pack)
    with jax.named_scope("a_swap"):
        other = lax.ppermute(after(mine, own, last), "col", SWAP)
    with jax.named_scope("b_plane"):
        b = plane_gather(after(slabs, mine))
    *solved, good = chain(place, mine, other)
    with jax.named_scope("c_swap"):
        far = lax.ppermute(after(own, good), "col", SWAP)
        last_far = lax.ppermute(after(last, good), "col", [(c, c + 1) for c in range(0, N, 2)])
    weights = rows(place, good, own, far, last, last_far, *solved)
    out = final(place, good, block, b, *weights)
    return out[None, :, None, :]


def solution(mesh):
    spec = P("row", None, "col", None)
    return jax.shard_map(on_device, mesh=mesh, in_specs=(spec,), out_specs=spec, check_vma=False)
```

```python
import jax
import jax.numpy as jnp
from jax import lax
from jax.experimental import pallas as pl
from jax.experimental.pallas import tpu as pltpu
from jax.sharding import PartitionSpec as P

TILE = 512
N = 16
SLAB = TILE // N
F32 = jnp.float32
BF16 = jnp.bfloat16
NN = (((1,), (0,)), ((), ()))
NT = (((1,), (1,)), ((), ()))
TN = (((0,), (0,)), ((), ()))


def halves(value):
    high = value.astype(BF16)
    return high, (value - high.astype(F32)).astype(BF16)


def dot1(left, right):
    return lax.dot_general(left.astype(BF16), right.astype(BF16), NN, preferred_element_type=F32)


def dot3(left, right, dims=NN):
    lh, ll = left if isinstance(left, tuple) else halves(left)
    rh, rl = right if isinstance(right, tuple) else halves(right)
    low = lax.dot_general(lh, rl, dims, preferred_element_type=F32)
    low += lax.dot_general(ll, rh, dims, preferred_element_type=F32)
    return low + lax.dot_general(lh, rh, dims, preferred_element_type=F32)


def eye_mask():
    rows = lax.broadcasted_iota(jnp.int32, (TILE, TILE), 0)
    cols = lax.broadcasted_iota(jnp.int32, (TILE, TILE), 1)
    return rows == cols


def sweep_inverse(mat, inv_ref):
    inv_ref[...] = mat
    rows = lax.broadcasted_iota(jnp.int32, (TILE, TILE), 0)
    cols = lax.broadcasted_iota(jnp.int32, (TILE, TILE), 1)

    def body(k, carry):
        cur = inv_ref[...]
        col = jnp.sum(jnp.where(cols == k, cur, 0.0), axis=1, keepdims=True)
        row = jnp.sum(jnp.where(rows == k, cur, 0.0), axis=0, keepdims=True)
        pivot = jnp.sum(jnp.where((cols == k) & (rows == k), cur, 0.0))
        rate = 1.0 / pivot
        new = cur - (col * rate) * row
        new = jnp.where(rows == k, row * rate, new)
        new = jnp.where(cols == k, col * rate, new)
        inv_ref[...] = jnp.where((rows == k) & (cols == k), -rate, new)
        return carry

    lax.fori_loop(0, TILE, body, 0)
    inv_ref[...] = -inv_ref[...]


def exact(left, right, dims=NN):
    return lax.dot_general(left, right, dims, precision=lax.Precision.HIGHEST, preferred_element_type=F32)


def same(value):
    return value


TOL = 1e-5


def quick_inverse(mat_ref, inv_ref, good):
    mat = mat_ref[...]
    diag = eye_mask()
    ident = jnp.where(diag, 1.0, 0.0).astype(F32)
    kept = jnp.where(diag, mat, 0.0)
    rate_c = 1.0 / jnp.sum(kept, axis=1, keepdims=True)
    rate_r = 1.0 / jnp.sum(kept, axis=0, keepdims=True)
    mat2 = halves(mat)
    inv = jnp.where(diag, rate_r, -(mat * rate_c) * rate_r)
    rest = ident - lax.dot_general(mat2[0], inv.astype(BF16), NN, preferred_element_type=F32)
    inv = inv + dot1(inv, rest)
    for _ in range(2):
        rest = ident - dot3(mat2, inv)
        inv = inv + dot1(inv, rest)
    inv_ref[...] = inv

    @pl.when(jnp.logical_not(jnp.sum(rest * rest) < TOL))
    def _():
        good[0] = 0


def chain_kernel(place, mine, other, *rest):
    outs, (good, mat, out_sems), kept = rest[:6], rest[6:9], rest[9:]
    x0, x1, x2, g10, g20, g21 = kept

    def tile(group, k):
        left, right = (mine, other) if group == 0 else (other, mine)
        return jnp.where(place[2] == 0, left[:, k], right[:, k]).reshape(TILE, TILE)

    def second(mm, split):
        a10 = split(tile(0, 1))
        g = mm(a10, split(x0[...]))
        g10[...] = g
        mat[...] = tile(1, 0) - mm(split(g), a10, NT)

    def third(mm, split):
        a10 = split(tile(0, 1))
        a20 = split(tile(0, 2))
        g = mm(a20, split(x0[...]))
        g20[...] = g
        g = split(g)
        s21 = split(tile(1, 1) - mm(g, a10, NT))
        mat[...] = tile(1, 2) - mm(g, a20, NT)
        g = mm(s21, split(x1[...]))
        g21[...] = g
        mat[...] -= mm(split(g), s21, NT)

    good[0] = 1
    mat[...] = tile(0, 0)
    quick_inverse(mat, x0, good)
    second(dot3, halves)
    quick_inverse(mat, x1, good)
    third(dot3, halves)
    quick_inverse(mat, x2, good)

    @pl.when(good[0] == 0)
    def _():
        sweep_inverse(tile(0, 0), x0)
        second(exact, same)
        sweep_inverse(mat[...], x1)
        third(exact, same)
        sweep_inverse(mat[...], x2)

    send = [pltpu.make_async_copy(kept[i], outs[i], out_sems.at[i]) for i in range(6)]
    for copy in send:
        copy.start()
    for copy in send:
        copy.wait()


def fetched(sources, scratch, sems):
    copies = [pltpu.make_async_copy(sources[i], scratch.at[i], sems.at[i]) for i in range(len(sources))]
    for copy in copies:
        copy.start()

    def get(i):
        copies[i].wait()
        return scratch.at[i]

    return get


def row_kernel(place, good, own, far, last, last_far, x0, x1, x2, g10, g20, g21, w0, w1, w2, hold, kept, sems, out_sems):
    row = place[0]
    first_core = place[2] == 0
    get = fetched([own, far, last, last_far, x0, g10, x1, g20, g21, x2], hold, sems)
    own, far, last, last_far, x0, g10, x1, g20, g21, x2 = [get(i) for i in range(10)]

    def finish(mm, split):
        ident = jnp.where(eye_mask(), 1.0, 0.0).astype(F32)

        def rowside(k):
            left, right = ((own, far), (far, own), (last, last_far))[k]
            value = jnp.where(first_core, left[...], right[...])
            return jnp.where(row < 3, jnp.where(row == k, -1.0, 0.0) * ident, value)

        g10h = split(g10[...])
        g20h = split(g20[...])
        g21h = split(g21[...])
        u0 = split(rowside(0))
        kept[0] = mm(u0, split(x0[...]))
        u1 = split(rowside(1) - mm(u0, g10h, NT))
        kept[1] = mm(u1, split(x1[...]))
        u2 = rowside(2) - mm(u0, g20h, NT) - mm(u1, g21h, NT)
        value = mm(split(u2), split(x2[...]))
        kept[2] = value
        part = split(value)
        kept[0] -= mm(part, g20h)
        value = kept[1] - mm(part, g21h)
        kept[1] = value
        kept[0] -= mm(split(value), g10h)

    @pl.when(good[0] == 1)
    def _():
        finish(dot3, halves)

    @pl.when(good[0] == 0)
    def _():
        finish(exact, same)

    send = [pltpu.make_async_copy(kept.at[i], out, out_sems.at[i]) for i, out in enumerate((w0, w1, w2))]
    for copy in send:
        copy.start()
    for copy in send:
        copy.wait()


def final_kernel(place, good, block, b, w0, w1, w2, out, hold, tiles, sems, tile_sems):
    row = place[0]
    col = place[1]
    fetch = [pltpu.make_async_copy(b.at[:, k], tiles.at[k], tile_sems.at[k]) for k in range(3)]
    for copy in fetch:
        copy.start()
    get = fetched([block, w0, w1, w2], hold, sems)
    block, w0, w1, w2 = [get(i) for i in range(4)]
    for copy in fetch:
        copy.wait()

    def finish(mm, split):
        ident = jnp.where(eye_mask(), 1.0, 0.0).astype(F32)

        def colside(k):
            value = tiles[k].reshape(TILE, TILE)
            return jnp.where(col < 3, jnp.where(col == k, 1.0, 0.0) * ident, value)

        total = jnp.where((row < 3) | (col < 3), 0.0, block[...])
        for k, weight in enumerate((w0, w1, w2)):
            total -= mm(split(weight[...]), split(colside(k)))
        out[...] = total

    @pl.when(good[0] == 1)
    def _():
        finish(dot3, halves)

    @pl.when(good[0] == 0)
    def _():
        finish(exact, same)


TILE_F32 = jax.ShapeDtypeStruct((TILE, TILE), F32)
VM = pl.BlockSpec(memory_space=pltpu.VMEM)
SM = pl.BlockSpec(memory_space=pltpu.SMEM)
ANY = pl.BlockSpec(memory_space=pl.ANY)
ROOM = pltpu.CompilerParams(vmem_limit_bytes=36 * 1024 * 1024)


def cost(products):
    return pl.CostEstimate(flops=products * 10**9, bytes_accessed=12 * 2**20, transcendentals=0)


def chain(*args):
    return pl.pallas_call(
        chain_kernel,
        out_shape=[TILE_F32] * 6 + [jax.ShapeDtypeStruct((1,), jnp.int32)],
        in_specs=[SM] + [VM] * 2,
        out_specs=[ANY] * 6 + [SM],
        scratch_shapes=[
            pltpu.VMEM((TILE, TILE), F32),
            pltpu.SemaphoreType.DMA((6,)),
        ]
        + [pltpu.VMEM((TILE, TILE), F32)] * 6,
        compiler_params=ROOM,
        cost_estimate=cost(20),
        name="chain",
    )(*args)


def rows(*args):
    return pl.pallas_call(
        row_kernel,
        out_shape=[TILE_F32] * 3,
        in_specs=[SM] * 2 + [ANY] * 10,
        out_specs=[ANY] * 3,
        scratch_shapes=[
            pltpu.VMEM((10, TILE, TILE), F32),
            pltpu.VMEM((3, TILE, TILE), F32),
            pltpu.SemaphoreType.DMA((10,)),
            pltpu.SemaphoreType.DMA((3,)),
        ],
        compiler_params=ROOM,
        cost_estimate=cost(13),
        name="rows",
    )(*args)


def final(*args):
    return pl.pallas_call(
        final_kernel,
        out_shape=TILE_F32,
        in_specs=[SM] * 2 + [ANY] * 5,
        out_specs=VM,
        scratch_shapes=[
            pltpu.VMEM((4, TILE, TILE), F32),
            pltpu.VMEM((3, N, SLAB, TILE), F32),
            pltpu.SemaphoreType.DMA((4,)),
            pltpu.SemaphoreType.DMA((3,)),
        ],
        compiler_params=ROOM,
        cost_estimate=cost(4),
        name="final",
    )(*args)


def line(pairs, cores):
    return [(2 * a % N + h, 2 * b % N + h) for a, b in pairs for h in cores]


def after(value, *earlier):
    return lax.optimization_barrier((value, earlier))[0]


def plane_gather(part):
    copies = jnp.broadcast_to(part[None], (N,) + part.shape)
    return lax.all_to_all(copies, "row", 0, 0, tiled=True)


SWAP = [(c, c ^ 1) for c in range(N)]


def line_send(value, root, cores=(0, 1)):
    fwd = lax.ppermute(value, "col", line([(root, root + 3)], cores))
    back = lax.ppermute(value, "col", line([(root, root + 5)], cores))
    return fwd, back


def line_start(value, z, root, sent):
    return jnp.where(z == root, value, sent[0] + sent[1])


def line_end(value, z, root, cores=(0, 1)):
    fwd = lax.ppermute(value, "col", line([(root + i, root + i + 1) for i in (0, 3, 5)], cores))
    back = lax.ppermute(value, "col", line([(root + i, root + i - 1) for i in (0, 3)], cores))
    have = (z == root) | (z == (root + 3) % 8) | (z == (root + 5) % 8)
    return jnp.where(have, value, fwd + back)


def on_device(fisher):
    block = fisher[0, :, 0, :]
    row = lax.axis_index("row")
    col = lax.axis_index("col")
    z, core = col // 2, col % 2
    place = jnp.stack([row, col, core]).astype(jnp.int32)

    with jax.named_scope("c_start"):
        own = line_send(block, 0)
        last = line_send(block, 1, (0,))
    with jax.named_scope("slabs"):
        slabs = lax.all_to_all(block, "row", 0, 0, tiled=True).reshape(N, SLAB, TILE)[:3]
    with jax.named_scope("a_line"):
        corner = lax.ppermute(slabs[2], "col", [(2, 1)])
        pack = jnp.where(col == 1, jnp.stack([slabs[1], slabs[2], corner]), slabs)
        seed = after(line_start(pack, z, 0, line_send(pack, 0)), own, last)
        pack = line_end(seed, z, 0)
    with jax.named_scope("c_end"):
        own, last = after((own, last), pack)
        own = line_end(line_start(block, z, 0, own), z, 0)
        last = line_end(line_start(block, z, 1, last), z, 1, (0,))
    with jax.named_scope("a_plane"):
        mine = plane_gather(pack)
    with jax.named_scope("a_swap"):
        other = lax.ppermute(after(mine, own, last), "col", SWAP)
    with jax.named_scope("b_plane"):
        b = plane_gather(after(slabs, mine))
    *solved, good = chain(place, mine, other)
    with jax.named_scope("c_swap"):
        far = lax.ppermute(after(own, good), "col", SWAP)
        last_far = lax.ppermute(after(last, good), "col", [(c, c + 1) for c in range(0, N, 2)])
    weights = rows(place, good, own, far, last, last_far, *solved)
    out = final(place, good, block, b, *weights)
    return out[None, :, None, :]


def solution(mesh):
    spec = P("row", None, "col", None)
    return jax.shard_map(on_device, mesh=mesh, in_specs=(spec,), out_specs=spec, check_vma=False)
```
